512 devices in a mesh: dp: 64 (over y, z), tensor: 8 (over x, core).
Axes of the slice: x: 4, y: 4, z: 16, core: 2. Of those that a mesh axis runs over, the one named last changes fastest.
Arguments:
- normed: bfloat16 [23552, 4096], P('dp', 'tensor'), may hold values from -6 to 6
- kv_cotangent: bfloat16 [2, 23552, 1024], P(None, 'dp', 'tensor'), may hold values from -6 to 6
- kv_weight: bfloat16 [2, 4096, 1024], P(None, 'dp', 'tensor'), may hold values from -0.25 to 0.25
- error_buffer: bfloat16 [64, 2, 4096, 1024], P('dp', None, None, 'tensor'), may hold values from -383.66652 to 383.66652
- q_factor: float32 [2, 16, 1024], P(None, None, 'tensor'), may hold values from -40 to 40
Outputs:
- input_grad: bfloat16 [23552, 4096], P('dp', 'tensor')
- approx: bfloat16 [2, 4096, 1024], P(None, 'dp', 'tensor')
- new_error: bfloat16 [64, 2, 4096, 1024], P('dp', None, None, 'tensor')
The draws below stay inside these ranges and needn't reach their ends.
All inputs are finite; a program needn't handle non-finite values.
Results may differ from the reference program's by a relative error of at most 0.018.
Values may be sent and summed in bfloat16 or wider, within the bound.
No kernel may reach another device: no remote copies, remote signals or barrier semaphores. Data moves between devices by JAX's collectives and lax.ppermute only.
A program may use at most 64 MiB of HBM per device.

```python
import math
import jax
import jax.numpy as jnp
from jax import lax

D = 4096
KVW = 1024
RANK = 16
TOK_DEV = 368
TOKENS = 23552
WORKERS = 64
N_DP = 64
N_TENSOR = 8


def draw_error_buffer(key, part):
    key = jax.random.fold_in(key, 3)
    shape = (WORKERS, 2, D, KVW)
    spread = jax.random.uniform(jax.random.fold_in(key, 1), (WORKERS, 2, D, 1), jnp.float32, 0.0, 1.0)
    row_scale = 0.5 * jnp.exp(spread * math.log(10.0))
    values = jax.random.truncated_normal(jax.random.fold_in(key, 2), -4.0, 4.0, shape, jnp.float32)
    return (TOK_DEV ** 0.5 * row_scale * values).astype(jnp.bfloat16)


def draw_q_factor(key, part):
    key = jax.random.fold_in(key, 5)
    spread = jax.random.uniform(jax.random.fold_in(key, 1), (2, RANK, 1), jnp.float32, 0.0, 1.0)
    column_scale = jnp.exp(spread * math.log(10.0))
    values = jax.random.truncated_normal(jax.random.fold_in(key, 2), -4.0, 4.0, (2, RANK, KVW), jnp.float32)
    return column_scale * values


def strengthened(result, key, source, target, shards_of, factor):
    def block_of(position):
        return (jnp.arange(result.shape[position]) // (result.shape[position] // shards_of)).reshape((-1,) + (1,) * (result.ndim - 1 - position))

    one_side = jax.random.permutation(key, shards_of)[block_of(target)]
    other_side = (block_of(target) + shards_of // 2) % shards_of
    return jnp.where((block_of(source) == one_side) | (block_of(source) == other_side), factor * result, result)


def shard_levels(stream_key, shape, pieces, low, largest):
    gain, own = 1.0, jax.random.fold_in(stream_key, 6)
    for dim, shards_of in pieces:
        heights = jnp.exp(jax.random.uniform(jax.random.fold_in(own, dim), (shards_of,), jnp.float32, low / len(pieces), largest / len(pieces)))
        gain = gain * jnp.repeat(heights, shape[dim] // shards_of).reshape([-1 if axis == dim else 1 for axis in range(len(shape))])
    return gain


def scatter_about(key, dims, scale, most, shards=(), kind=jnp.bfloat16):
    drawn = jax.random.normal(key, dims, jnp.float32) * scale
    if len(shards) > 0:
        drawn = shard_levels(key, dims, shards, -0.22, 0.18) * drawn
    return jnp.clip(drawn, min=-most, max=most).astype(kind)


def gaussian_with(key, dims, deviation, limit, pieces, heavy, kind=jnp.bfloat16):
    entries = deviation * jax.random.normal(key, dims, jnp.float32)
    if pieces:
        entries = entries * shard_levels(key, dims, pieces, -0.22, 0.18)
    return jnp.clip(strengthened(entries, jax.random.fold_in(key, 3), *heavy), -limit, limit).astype(kind)


def setup_inputs(seed: int = 0) -> dict:
    key_list = jax.random.split(jax.random.key(seed), 6)
    normed = scatter_about(key_list[0], (TOKENS, D), 1.0, 6.0, ((0, 64), (1, 8)))
    kv_cotangent = scatter_about(key_list[1], (2, TOKENS, KVW), 1.0, 6.0, ((1, 64), (2, 8)))
    kv_weight = gaussian_with(key_list[2], (2, D, KVW), D ** -0.5, 0.25, ((1, 64), (2, 8)), (2, 1, 64, 4.0))
    error_buffer = draw_error_buffer(jax.random.fold_in(key_list[5], 71), 0)
    q_factor = draw_q_factor(jax.random.fold_in(key_list[5], 71), 0)
    return dict(normed=normed, kv_cotangent=kv_cotangent, kv_weight=kv_weight, error_buffer=error_buffer, q_factor=q_factor)


EPSILON = 1e-06

def orthonormal(p_sum):
    highest = lax.Precision.HIGHEST
    basis_cols = jnp.zeros_like(p_sum)
    for column in range(RANK):
        vector = p_sum[:, column]
        coeffs = jnp.einsum('kid,kd->ki', basis_cols, vector, precision=highest)
        vector = vector - jnp.einsum('ki,kid->kd', coeffs, basis_cols, precision=highest)
        length = jnp.sqrt(lax.optimization_barrier(jnp.sum(vector * vector, axis=-1)) + EPSILON)
        basis_cols = basis_cols.at[:, column].set(vector / length[:, None])
    return basis_cols

def reference(normed, kv_cotangent, kv_weight, error_buffer, q_factor):
    highest = lax.Precision.HIGHEST
    width = KVW // N_TENSOR

    def input_part(running, block_index):
        first_col = block_index * width
        cot_block = lax.dynamic_slice_in_dim(kv_cotangent, first_col, width, 2).astype(jnp.float32)
        weight_block = lax.dynamic_slice_in_dim(kv_weight, first_col, width, 2).astype(jnp.float32)
        partial_value = jnp.einsum('ktc,kdc->td', cot_block, weight_block).astype(jnp.bfloat16)
        partial_value = lax.optimization_barrier(partial_value)
        return (running + partial_value.astype(jnp.float32), None)
    input_total, _ = lax.scan(input_part, jnp.zeros((TOKENS, D), jnp.float32), jnp.arange(N_TENSOR, dtype=jnp.int32))
    input_grad = input_total.astype(jnp.bfloat16)
    worker_ids = jnp.arange(N_DP, dtype=jnp.int32)

    def worker_data(worker):
        first_row = worker * TOK_DEV
        feature_rows = lax.dynamic_slice_in_dim(normed, first_row, TOK_DEV, 0).astype(jnp.float32)
        cotangent = lax.dynamic_slice_in_dim(kv_cotangent, first_row, TOK_DEV, 1).astype(jnp.float32)
        errors = lax.dynamic_index_in_dim(error_buffer, worker, 0, keepdims=False).astype(jnp.float32)
        return (feature_rows, cotangent, errors)

    def p_part(running, worker):
        feature_rows, cotangent, errors = worker_data(worker)
        reduced = jnp.einsum('ktc,krc->ktr', cotangent, q_factor, precision=highest)
        worker_term = jnp.einsum('td,ktr->krd', feature_rows, reduced, precision=highest)
        worker_term = worker_term + jnp.einsum('kdc,krc->krd', errors, q_factor, precision=highest)
        return (running + worker_term, None)
    p_total, _ = lax.scan(p_part, jnp.zeros((2, RANK, D), jnp.float32), worker_ids)
    basis_cols = orthonormal(p_total / N_DP)

    def q_part(running, worker):
        feature_rows, cotangent, errors = worker_data(worker)
        reduced = jnp.einsum('td,krd->ktr', feature_rows, basis_cols, precision=highest)
        worker_term = jnp.einsum('ktr,ktc->krc', reduced, cotangent, precision=highest)
        worker_term = worker_term + jnp.einsum('krd,kdc->krc', basis_cols, errors, precision=highest)
        return (running + worker_term, None)
    q_total, _ = lax.scan(q_part, jnp.zeros((2, RANK, KVW), jnp.float32), worker_ids)
    q_total = q_total / N_DP
    approx_full = jnp.einsum('krd,krc->kdc', basis_cols, q_total, precision=highest)

    def error_part(worker):
        feature_rows, cotangent, errors = worker_data(worker)
        gradient = jnp.einsum('td,ktc->kdc', feature_rows, cotangent)
        return (gradient + errors - approx_full).astype(jnp.bfloat16)
    new_error = lax.map(error_part, worker_ids)
    return (input_grad, approx_full.astype(jnp.bfloat16), new_error)
```

```python
import jax
import jax.numpy as jnp
from jax import lax
from jax.experimental import pallas as pl
from jax.experimental.pallas import tpu as pltpu
from jax.sharding import Mesh
from jax.sharding import PartitionSpec as P

EPSILON = 1e-06
WORKERS = 64
NY, NZ, NX, NC = 4, 16, 4, 2
NT = NX * NC
RANK = 16
ROWS = 2 * RANK
D = 4096
BLK = D // NT
TOK = 368
TOKP = 384
COL = 128
GCOL = BLK + 2 * COL
F32 = jnp.float32
BF16 = jnp.bfloat16
VMEM = pl.BlockSpec(memory_space=pltpu.VMEM)
SMEM = pl.BlockSpec(memory_space=pltpu.SMEM)
NT_DIMS = (((1,), (1,)), ((), ()))
NN_DIMS = (((1,), (0,)), ((), ()))
TN_DIMS = (((0,), (0,)), ((), ()))


def dot(a, b, dims):
    return lax.dot_general(a, b, dims, preferred_element_type=F32)


def pieces(value, count):
    result = []
    for _ in range(count):
        part = value.astype(BF16)
        result.append(part)
        value = value - part.astype(F32)
    return result


def call(kernel, out_shape, *args, scratch=(), specs=None, flops=0, moved=0):
    outs = jax.tree.map(lambda _: VMEM, out_shape)
    return pl.pallas_call(
        kernel,
        out_shape=out_shape,
        in_specs=specs or [VMEM] * len(args),
        out_specs=outs,
        scratch_shapes=list(scratch),
        compiler_params=pltpu.CompilerParams(vmem_limit_bytes=24 * 2**20),
        cost_estimate=pl.CostEstimate(flops=flops, bytes_accessed=moved, transcendentals=0),
    )(*args)


def shape(dims, dtype=F32):
    return jax.ShapeDtypeStruct(dims, dtype)


def first_kernel(error_ref, cot_ref, q_ref, out_ref):
    out_ref[:, :, BLK + TOKP - 128 :] = jnp.zeros((NT, ROWS, 128), F32)
    for k in range(2):
        rows = slice(RANK * k, RANK * (k + 1))
        q = jnp.concatenate(pieces(q_ref[k], 3), axis=0)
        token = dot(q, cot_ref[k], NT_DIMS)
        token = token[:RANK] + token[RANK : 2 * RANK] + token[2 * RANK :]
        for t in range(NT):
            part = dot(q, error_ref[k, BLK * t : BLK * (t + 1), :], NT_DIMS)
            out_ref[t, rows, :BLK] = part[:RANK] + part[RANK : 2 * RANK] + part[2 * RANK :]
            out_ref[t, rows, BLK : BLK + TOK] = token


def second_kernel(recv_ref, normed_ref, weight_ref, out_ref):
    total = recv_ref[0]
    for t in range(1, NT):
        total = total + recv_ref[t]
    token = jnp.concatenate(pieces(total[:, BLK : BLK + TOK], 3), axis=0)
    grad = dot(token, normed_ref[...], NN_DIMS)
    factor = total[:, :BLK] + (grad[:ROWS] + grad[ROWS : 2 * ROWS] + grad[2 * ROWS :])
    weight = jnp.concatenate([weight_ref[0], weight_ref[1]], axis=1).astype(F32)
    weight = jnp.concatenate([weight[:32], weight[32:]], axis=1)
    for y in range(NY):
        out_ref[y, :8, :] = factor[8 * y : 8 * y + 8]
        out_ref[y, 8:, :] = weight


def third_kernel(recv_ref, out_ref, weight_ref):
    total = (recv_ref[0, :8] + recv_ref[1, :8]) + (recv_ref[2, :8] + recv_ref[3, :8])
    for z in range(NZ):
        out_ref[z] = total
    for y in range(NY):
        weight = recv_ref[y, 8:, :]
        weight_ref[y] = jnp.concatenate([weight[:, :256], weight[:, 256:]], axis=0).astype(BF16)


def repeat_kernel(scale, recv_ref, out_ref):
    total = recv_ref[0]
    for i in range(1, recv_ref.shape[0]):
        total = total + recv_ref[i]
    total = total * scale
    for i in range(out_ref.shape[0]):
        out_ref[i] = total


def basis_kernel(recv_ref, gathered_ref, cot_ref, error_ref, basis_ref, term_ref, p_ref, v_ref):
    for y in range(NY):
        for t in range(NT):
            block = recv_ref[NT * y + t]
            p_ref[8 * y : 8 * y + 8, BLK * t : BLK * (t + 1)] = block
            v_ref[8 * y : 8 * y + 8, BLK * t : BLK * (t + 1)] = block
    for i in range(RANK):
        for k in range(2):
            row = RANK * k + i
            vector = v_ref[row : row + 1, :]
            square = jnp.sum(vector * vector, axis=1, keepdims=True) + EPSILON
            inverse = 1.0 / jnp.sqrt(square)
            column = vector * inverse
            basis_ref[row : row + 1, :] = column
            if i < RANK - 1:
                low = RANK * k + 8 * ((i + 1) // 8)
                rows = slice(low, RANK * (k + 1))
                coeff = jnp.sum(p_ref[rows, :] * column, axis=1, keepdims=True)
                v_ref[rows, :] = v_ref[rows, :] - coeff * column
    basis = [jnp.concatenate(pieces(basis_ref[RANK * k : RANK * (k + 1), :], 3), axis=0) for k in range(2)]
    both = jnp.concatenate(basis, axis=0)
    token = jnp.zeros((96, TOK), F32)
    for t in range(NT):
        token = token + dot(
            both[:, BLK * t : BLK * (t + 1)], gathered_ref[:, GCOL * t : GCOL * t + BLK], NT_DIMS
        )
    for k in range(2):
        reduced = token[48 * k : 48 * k + 16] + token[48 * k + 16 : 48 * k + 32] + token[48 * k + 32 : 48 * k + 48]
        reduced = jnp.concatenate(pieces(reduced, 3), axis=0)
        term = dot(reduced, cot_ref[k], NN_DIMS) + dot(basis[k], error_ref[k], NN_DIMS)
        term = term[:RANK] + term[RANK : 2 * RANK] + term[2 * RANK :]
        for z in range(NZ):
            term_ref[z, RANK * k : RANK * (k + 1), :] = term


def final_kernel(worker_ref, recv_ref, basis_ref, gathered_ref, cot_ref, error_ref, approx_ref, new_ref, tile_ref):
    q_total = (recv_ref[0] + recv_ref[1]) + (recv_ref[2] + recv_ref[3])
    q_total = q_total * (1.0 / WORKERS)
    zero = jnp.zeros((RANK, COL), BF16)
    right = []
    for k in range(2):
        q1, q2 = pieces(q_total[RANK * k : RANK * (k + 1)], 2)
        for q in (q1, q2, q1):
            right.append(jnp.concatenate([q, zero] if k == 0 else [zero, q], axis=1))
    right = jnp.concatenate(right, axis=0)
    cot = jnp.concatenate([cot_ref[0], cot_ref[1]], axis=1)

    def left_of(columns):
        left = []
        for k in range(2):
            b1, b2 = pieces(basis_ref[RANK * k : RANK * (k + 1), columns], 2)
            left += [b1, b1, b2]
        return jnp.concatenate(left, axis=0)

    worker = worker_ref[0]
    first = pl.multiple_of((worker // 2) * 128, 128)
    tile_ref[...] = dot(left_of(pl.ds(first, 128)), right, TN_DIMS)
    mine = tile_ref[pl.ds(pl.multiple_of((worker % 2) * 64, 64), 64), :]
    approx_ref[0] = mine[:, :COL].astype(BF16)
    approx_ref[1] = mine[:, COL:].astype(BF16)

    minus = jnp.concatenate([cot, -right], axis=0)
    for t in range(NT):
        left = jnp.concatenate(
            [gathered_ref[:, GCOL * t : GCOL * t + BLK], left_of(slice(BLK * t, BLK * (t + 1)))], axis=0
        )
        value = dot(left, minus, TN_DIMS)
        for k in range(2):
            rows = slice(BLK * t, BLK * (t + 1))
            error = error_ref[k, rows, :].astype(F32)
            new_ref[k, rows, :] = (value[:, COL * k : COL * (k + 1)] + error).astype(BF16)


def input_kernel(core_ref, gathered_ref, weight_ref, keep_ref, send_ref):
    core = core_ref[0]
    for own in range(2):
        half = core if own else 1 - core
        total = jnp.zeros((TOK, BLK), F32)
        for x in range(NX):
            first = pl.multiple_of((NC * x + core) * GCOL + BLK, 128)
            cot = gathered_ref[:, pl.ds(first, 2 * COL)]
            weight = weight_ref[pl.ds(half * 8, 8), x].reshape(BLK, 2 * COL)
            total = total + dot(cot, weight, NT_DIMS)
        if own:
            keep_ref[...] = total
        else:
            send_ref[...] = total.astype(BF16)


def add_kernel(keep_ref, recv_ref, out_ref):
    out_ref[...] = (keep_ref[...] + recv_ref[...].astype(F32)).astype(BF16)


def exchange(value, axes):
    return lax.all_to_all(value, axes, 0, 0, tiled=True)


def shards(normed, kv_cotangent, kv_weight, error_buffer, q_factor):
    error = error_buffer[0]
    local = jnp.concatenate([normed, kv_cotangent[0], kv_cotangent[1]], axis=1)
    gathered = lax.all_gather(local, ("x", "core"), axis=1, tiled=True)

    sent = call(first_kernel, shape((NT, ROWS, BLK + TOKP)), error, kv_cotangent, q_factor)
    sent = call(second_kernel, shape((NY, 40, BLK)), exchange(sent, ("x", "core")), normed, kv_weight)
    sent, weight = call(
        third_kernel, (shape((NZ, 8, BLK)), shape((NY, 64, 2 * COL), BF16)), exchange(sent, ("y",))
    )
    weight = exchange(weight, ("x",))
    weight = lax.all_gather(weight, "z", axis=0, tiled=False)
    sent = call(
        lambda *refs: repeat_kernel(1.0 / WORKERS, *refs), shape((NY * NT, 8, BLK)), exchange(sent, ("z",))
    )
    recv = exchange(sent, ("y", "x", "core"))
    basis, term = call(
        basis_kernel,
        (shape((ROWS, D)), shape((NZ, ROWS, COL))),
        recv,
        gathered,
        kv_cotangent,
        error,
        scratch=[pltpu.VMEM((ROWS, D), F32), pltpu.VMEM((ROWS, D), F32)],
    )
    term = call(lambda *refs: repeat_kernel(1.0, *refs), shape((NY, ROWS, COL)), exchange(term, ("z",)))
    term = exchange(term, ("y",))
    worker = lax.axis_index(("y", "z")).astype(jnp.int32).reshape(1)
    approx, new_error = call(
        final_kernel,
        (shape((2, 64, COL), BF16), shape((2, D, COL), BF16)),
        worker,
        term,
        basis,
        gathered,
        kv_cotangent,
        error,
        scratch=[pltpu.VMEM((COL, 2 * COL), F32)],
        specs=[SMEM] + [VMEM] * 5,
    )
    core = lax.axis_index("core").astype(jnp.int32).reshape(1)
    approx, weight = lax.optimization_barrier((approx, weight))
    keep, give = call(
        input_kernel,
        (shape((TOK, BLK)), shape((TOK, BLK), BF16)),
        core,
        gathered,
        weight,
        specs=[SMEM, VMEM, VMEM],
    )
    take = lax.ppermute(give, "core", [(0, 1), (1, 0)])
    input_grad = call(add_kernel, shape((TOK, BLK), BF16), keep, take)
    return (input_grad, approx, new_error[None])


def solution(mesh):
    whole = Mesh(mesh.devices.reshape(NY, NZ, NX, NC), ("y", "z", "x", "core"))
    dp, tensor = ("y", "z"), ("x", "core")
    in_specs = (
        P(dp, tensor),
        P(None, dp, tensor),
        P(None, dp, tensor),
        P(dp, None, None, tensor),
        P(None, None, tensor),
    )
    out_specs = (P(dp, tensor), P(None, dp, tensor), P(dp, None, None, tensor))
    return jax.shard_map(shards, mesh=whole, in_specs=in_specs, out_specs=out_specs, check_vma=False)
```

```python
import jax
import jax.numpy as jnp
from jax import lax
from jax.experimental import pallas as pl
from jax.experimental.pallas import tpu as pltpu
from jax.sharding import Mesh
from jax.sharding import PartitionSpec as P

EPSILON = 1e-06
WORKERS = 64
NY, NZ, NX, NC = 4, 16, 4, 2
NT = NX * NC
RANK = 16
ROWS = 2 * RANK
D = 4096
BLK = D // NT
TOK = 368
TOKP = 384
COL = 128
GCOL = BLK + 2 * COL
F32 = jnp.float32
BF16 = jnp.bfloat16
VMEM = pl.BlockSpec(memory_space=pltpu.VMEM)
SMEM = pl.BlockSpec(memory_space=pltpu.SMEM)
HBM = pl.BlockSpec(memory_space=pl.ANY)
NT_DIMS = (((1,), (1,)), ((), ()))
NN_DIMS = (((1,), (0,)), ((), ()))
TN_DIMS = (((0,), (0,)), ((), ()))


def dot(a, b, dims):
    return lax.dot_general(a, b, dims, preferred_element_type=F32)


def pieces(value, count):
    result = []
    for _ in range(count):
        part = value.astype(BF16)
        result.append(part)
        value = value - part.astype(F32)
    return result


def call(kernel, out_shape, *args, scratch=(), specs=None, outs=None, flops=0, moved=0):
    return pl.pallas_call(
        kernel,
        out_shape=out_shape,
        in_specs=specs or [VMEM] * len(args),
        out_specs=outs or jax.tree.map(lambda _: VMEM, out_shape),
        scratch_shapes=list(scratch),
        compiler_params=pltpu.CompilerParams(vmem_limit_bytes=24 * 2**20),
        cost_estimate=pl.CostEstimate(flops=flops, bytes_accessed=moved, transcendentals=0),
    )(*args)


def shape(dims, dtype=F32):
    return jax.ShapeDtypeStruct(dims, dtype)


def tall(value):
    return jnp.concatenate([value[:, 128 * j : 128 * (j + 1)] for j in range(value.shape[1] // 128)], axis=0)


def wide(value, rows):
    return jnp.concatenate([value[rows * j : rows * (j + 1)] for j in range(value.shape[0] // rows)], axis=1)


def added(ref, rows=slice(None)):
    total = ref[0, rows]
    for i in range(1, ref.shape[0]):
        total = total + ref[i, rows]
    return total


def block(t):
    return slice(BLK * t, BLK * (t + 1))


def first_kernel(error_hbm, normed_hbm, cot_hbm, cot_ref, q_ref, out_ref, error_ref, local_hbm, sems, local_sems):
    copies = [
        pltpu.make_async_copy(error_hbm.at[:, block(t), :], error_ref.at[:, block(t), :], sems.at[t])
        for t in range(NT)
    ]
    for copy in copies:
        copy.start()
    local = [pltpu.make_async_copy(normed_hbm, local_hbm.at[:, :BLK], local_sems.at[2])]
    for k in range(2):
        columns = slice(BLK + COL * k, BLK + COL * (k + 1))
        local.append(pltpu.make_async_copy(cot_hbm.at[k], local_hbm.at[:, columns], local_sems.at[k]))
    for copy in local:
        copy.start()
    q = [jnp.concatenate(pieces(q_ref[k], 3), axis=0) for k in range(2)]
    for k in range(2):
        token = dot(q[k], cot_ref[k], NT_DIMS)
        token = token[:RANK] + token[RANK : 2 * RANK] + token[2 * RANK :]
        token = jnp.concatenate([token, jnp.zeros((RANK, TOKP - TOK), F32)], axis=1)
        for t in range(NT):
            for j in range(3):
                first = ROWS * (4 + j) + RANK * k
                out_ref[t, first : first + RANK, :] = token[:, 128 * j : 128 * (j + 1)]
    for t in range(NT):
        copies[t].wait()
        for k in range(2):
            part = dot(q[k], error_ref[k, block(t), :], NT_DIMS)
            part = part[:RANK] + part[RANK : 2 * RANK] + part[2 * RANK :]
            for j in range(4):
                first = ROWS * j + RANK * k
                out_ref[t, first : first + RANK, :] = part[:, 128 * j : 128 * (j + 1)]
    for copy in local:
        copy.wait()


def second_kernel(recv_ref, normed_ref, out_ref):
    total = added(recv_ref)
    token = jnp.concatenate(pieces(wide(total[4 * ROWS :], ROWS)[:, :TOK], 3), axis=0)
    grad = dot(token, normed_ref[...], NN_DIMS)
    factor = wide(total[: 4 * ROWS], ROWS) + (grad[:ROWS] + grad[ROWS : 2 * ROWS] + grad[2 * ROWS :])
    for y in range(NY):
        out_ref[y] = tall(factor[8 * y : 8 * y + 8])


def third_kernel(recv_ref, weight_ref, out_ref):
    total = added(recv_ref)
    weight = [weight_ref[k].astype(F32) for k in range(2)]
    for z in range(NZ):
        out_ref[z, :32, :] = total
        for k in range(2):
            out_ref[z, 32 + 64 * k : 96 + 64 * k, :] = weight[k]


def fourth_kernel(recv_ref, out_ref, weight_ref):
    total = added(recv_ref, slice(0, 32)) * (1.0 / WORKERS)
    for i in range(NY * NT):
        out_ref[i] = total
    for z in range(NZ):
        weight_ref[z] = recv_ref[z, 32:, :].astype(BF16)


def basis_kernel(
    recv_ref, gathered_hbm, cot_ref, error_ref, basis_ref, term_ref, features_ref, p_ref, v_ref, sems
):
    copies = [
        pltpu.make_async_copy(
            gathered_hbm.at[:, GCOL * t : GCOL * t + BLK], features_ref.at[t], sems.at[t]
        )
        for t in range(NT)
    ]
    for copy in copies:
        copy.start()
    for y in range(NY):
        for t in range(NT):
            value = wide(recv_ref[NT * y + t], 8)
            p_ref[8 * y : 8 * y + 8, block(t)] = value
            v_ref[8 * y : 8 * y + 8, block(t)] = value
    for i in range(RANK):
        for k in range(2):
            row = RANK * k + i
            vector = v_ref[row : row + 1, :]
            square = jnp.sum(vector * vector, axis=1, keepdims=True) + EPSILON
            column = vector * (1.0 / jnp.sqrt(square))
            basis_ref[row : row + 1, :] = column
            if i < RANK - 1:
                rows = slice(RANK * k + 8 * ((i + 1) // 8), RANK * (k + 1))
                coeff = jnp.sum(p_ref[rows, :] * column, axis=1, keepdims=True)
                v_ref[rows, :] = v_ref[rows, :] - coeff * column
    basis = [
        jnp.concatenate(pieces(basis_ref[RANK * k : RANK * (k + 1), :], 3), axis=0) for k in range(2)
    ]
    both = jnp.concatenate(basis, axis=0)
    token = jnp.zeros((96, TOK), F32)
    for t in range(NT):
        copies[t].wait()
        token = token + dot(both[:, block(t)], features_ref[t], NT_DIMS)
    for k in range(2):
        part = token[48 * k : 48 * (k + 1)]
        part = part[:RANK] + part[RANK : 2 * RANK] + part[2 * RANK :]
        part = jnp.concatenate(pieces(part, 3), axis=0)
        term = dot(part, cot_ref[k], NN_DIMS) + dot(basis[k], error_ref[k], NN_DIMS)
        term = term[:RANK] + term[RANK : 2 * RANK] + term[2 * RANK :]
        for z in range(NZ):
            term_ref[z, RANK * k : RANK * (k + 1), :] = term


def repeat_kernel(recv_ref, out_ref):
    total = added(recv_ref)
    for i in range(out_ref.shape[0]):
        out_ref[i] = total


def final_kernel(
    worker_ref,
    recv_ref,
    basis_ref,
    features_ref,
    cot_ref,
    error_ref,
    approx_ref,
    new_hbm,
    tile_ref,
    new_ref,
    sems,
):
    q_total = added(recv_ref) * (1.0 / WORKERS)
    zero = jnp.zeros((RANK, COL), BF16)
    right = []
    for k in range(2):
        q1, q2 = pieces(q_total[RANK * k : RANK * (k + 1)], 2)
        for q in (q1, q2, q1):
            right.append(jnp.concatenate([q, zero] if k == 0 else [zero, q], axis=1))
    right = jnp.concatenate(right, axis=0)
    cot = jnp.concatenate([cot_ref[0], cot_ref[1]], axis=1)

    def left_of(columns):
        left = []
        for k in range(2):
            b1, b2 = pieces(basis_ref[RANK * k : RANK * (k + 1), columns], 2)
            left += [b1, b1, b2]
        return jnp.concatenate(left, axis=0)

    minus = jnp.concatenate([cot, -right], axis=0)
    copies = []
    for t in range(NT):
        left = jnp.concatenate([features_ref[t], left_of(block(t))], axis=0)
        value = dot(left, minus, TN_DIMS)
        for k in range(2):
            error = error_ref[k, block(t), :].astype(F32)
            new_ref[k, block(t), :] = (value[:, COL * k : COL * (k + 1)] + error).astype(BF16)
        copy = pltpu.make_async_copy(new_ref.at[:, block(t), :], new_hbm.at[:, block(t), :], sems.at[t])
        copy.start()
        copies.append(copy)

    worker = worker_ref[0]
    first = pl.multiple_of((worker // 2) * 128, 128)
    tile_ref[...] = dot(left_of(pl.ds(first, 128)), right, TN_DIMS)
    mine = tile_ref[pl.ds(pl.multiple_of((worker % 2) * 64, 64), 64), :]
    approx_ref[0] = mine[:, :COL].astype(BF16)
    approx_ref[1] = mine[:, COL:].astype(BF16)
    for copy in copies:
        copy.wait()


def half_product(core, half, gathered_hbm, weight_hbm, cot_ref, part_ref, sems):
    copies = []
    for x in range(NX):
        first = pl.multiple_of((NC * x + core) * GCOL + BLK, 128)
        copies.append(
            (
                pltpu.make_async_copy(gathered_hbm.at[:, pl.ds(first, 2 * COL)], cot_ref.at[x], sems.at[0, x]),
                pltpu.make_async_copy(weight_hbm.at[x, pl.ds(half * 8, 8)], part_ref.at[x], sems.at[1, x]),
            )
        )
    for one, other in copies:
        one.start()
        other.start()
    total = jnp.zeros((TOK, BLK), F32)
    for x in range(NX):
        for copy in copies[x]:
            copy.wait()
        weight = [part_ref[x, :, 64 * k : 64 * (k + 1), :].reshape(BLK, COL) for k in range(2)]
        total = total + dot(cot_ref[x], jnp.concatenate(weight, axis=1), NT_DIMS)
    return total


def give_kernel(core_ref, gathered_hbm, weight_hbm, out_ref, cot_ref, part_ref, sems):
    core = core_ref[0]
    out_ref[...] = half_product(core, 1 - core, gathered_hbm, weight_hbm, cot_ref, part_ref, sems).astype(BF16)


def keep_kernel(core_ref, gathered_hbm, weight_hbm, take_ref, out_ref, cot_ref, part_ref, sems):
    core = core_ref[0]
    total = half_product(core, core, gathered_hbm, weight_hbm, cot_ref, part_ref, sems)
    out_ref[...] = (total + take_ref[...].astype(F32)).astype(BF16)


def exchange(value, axes):
    return lax.all_to_all(value, axes, 0, 0, tiled=True)


def shards(normed, kv_cotangent, kv_weight, error_buffer, q_factor):
    dma = pltpu.SemaphoreType.DMA
    swap = [(NX * i + j, NX * j + i) for i in range(NY) for j in range(NX)]
    weight = lax.ppermute(kv_weight, ("y", "x"), swap)
    sent, error, local = call(
        first_kernel,
        (shape((NT, 7 * ROWS, 128)), shape((2, D, COL), BF16), shape((TOK, GCOL), BF16)),
        error_buffer[0],
        normed,
        kv_cotangent,
        kv_cotangent,
        q_factor,
        specs=[HBM, HBM, HBM, VMEM, VMEM],
        outs=(VMEM, VMEM, HBM),
        scratch=[dma((NT,)), dma((3,))],
    )
    recv = exchange(sent, ("x", "core"))
    recv, local = lax.optimization_barrier((recv, local))
    gathered = lax.all_gather(local, ("x", "core"), axis=1, tiled=True)
    recv = exchange(call(second_kernel, shape((NY, 32, 128)), recv, normed), ("y",))
    recv = exchange(call(third_kernel, shape((NZ, 160, 128)), recv, weight), ("z",))
    sent, weight = call(fourth_kernel, (shape((NY * NT, 32, 128)), shape((NZ, 128, 128), BF16)), recv)
    weight = lax.all_gather(weight, "y", axis=0, tiled=False)
    basis, term, features = call(
        basis_kernel,
        (shape((ROWS, D)), shape((NZ, ROWS, COL)), shape((NT, TOK, BLK), BF16)),
        exchange(sent, ("y", "x", "core")),
        gathered,
        kv_cotangent,
        error,
        specs=[VMEM, HBM, VMEM, VMEM],
        scratch=[pltpu.VMEM((ROWS, D), F32), pltpu.VMEM((ROWS, D), F32), dma((NT,))],
    )
    term = exchange(call(repeat_kernel, shape((NY, ROWS, COL)), exchange(term, ("z",))), ("y",))
    term, weight = lax.optimization_barrier((term, weight))
    core = lax.axis_index("core").astype(jnp.int32).reshape(1)
    product_scratch = [
        pltpu.VMEM((NX, TOK, 2 * COL), BF16),
        pltpu.VMEM((NX, 8, 128, COL), BF16),
        dma((2, NX)),
    ]
    give = call(
        give_kernel,
        shape((TOK, BLK), BF16),
        core,
        gathered,
        weight,
        specs=[SMEM, HBM, HBM],
        scratch=product_scratch,
    )
    take = lax.ppermute(give, "core", [(0, 1), (1, 0)])
    term, give = lax.optimization_barrier((term, give))
    worker = lax.axis_index(("y", "z")).astype(jnp.int32).reshape(1)
    approx, new_error = call(
        final_kernel,
        (shape((2, 64, COL), BF16), shape((2, D, COL), BF16)),
        worker,
        term,
        basis,
        features,
        kv_cotangent,
        error,
        specs=[SMEM] + [VMEM] * 5,
        outs=(VMEM, HBM),
        scratch=[pltpu.VMEM((COL, 2 * COL), F32), pltpu.VMEM((2, D, COL), BF16), dma((NT,))],
    )
    approx, take = lax.optimization_barrier((approx, take))
    input_grad = call(
        keep_kernel,
        shape((TOK, BLK), BF16),
        core,
        gathered,
        weight,
        take,
        specs=[SMEM, HBM, HBM, VMEM],
        scratch=product_scratch,
    )
    return (input_grad, approx, new_error[None])


def solution(mesh):
    whole = Mesh(mesh.devices.reshape(NY, NZ, NX, NC), ("y", "z", "x", "core"))
    dp, tensor = ("y", "z"), ("x", "core")
    in_specs = (
        P(dp, tensor),
        P(None, dp, tensor),
        P(None, dp, tensor),
        P(dp, None, None, tensor),
        P(None, None, tensor),
    )
    out_specs = (P(dp, tensor), P(None, dp, tensor), P(dp, None, None, tensor))
    return jax.shard_map(shards, mesh=whole, in_specs=in_specs, out_specs=out_specs, check_vma=False)
```

```python
import functools

import jax
import jax.numpy as jnp
from jax import lax
from jax.experimental import pallas as pl
from jax.experimental.pallas import tpu as pltpu
from jax.sharding import Mesh
from jax.sharding import PartitionSpec as P

EPSILON = 1e-06
WORKERS = 64
NY, NH, NL, NX, NC = 4, 8, 2, 4, 2
NT = NX * NC
NM = NY * NL
NZ = NH * NL
BIG = 59 * 2**20
RANK = 16
ROWS = 2 * RANK
D = 4096
BLK = D // NT
TOK = 368
TOKP = 384
COL = 128
GCOL = BLK + 2 * COL
F32 = jnp.float32
BF16 = jnp.bfloat16
VMEM = pl.BlockSpec(memory_space=pltpu.VMEM)
SMEM = pl.BlockSpec(memory_space=pltpu.SMEM)
HBM = pl.BlockSpec(memory_space=pltpu.HBM)
NT_DIMS = (((1,), (1,)), ((), ()))
NN_DIMS = (((1,), (0,)), ((), ()))
TN_DIMS = (((0,), (0,)), ((), ()))


def dot(a, b, dims):
    return lax.dot_general(a, b, dims, preferred_element_type=F32)


def pieces(value, count):
    result = []
    for _ in range(count):
        part = value.astype(BF16)
        result.append(part)
        value = value - part.astype(F32)
    return result


def call(kernel, out_shape, *args, scratch=(), specs=None, outs=None, cost=None, limit=16 * 2**20):
    return pl.pallas_call(
        kernel,
        out_shape=out_shape,
        in_specs=specs or [VMEM] * len(args),
        out_specs=outs or jax.tree.map(lambda _: VMEM, out_shape),
        scratch_shapes=list(scratch),
        cost_estimate=cost and pl.CostEstimate(flops=cost[0], bytes_accessed=cost[1], transcendentals=0),
        compiler_params=pltpu.CompilerParams(vmem_limit_bytes=limit),
    )(*args)


def shape(dims, dtype=F32):
    return jax.ShapeDtypeStruct(dims, dtype)


def tall(value):
    return jnp.concatenate([value[:, 128 * j : 128 * (j + 1)] for j in range(value.shape[1] // 128)], axis=0)


def wide(value, rows):
    return jnp.concatenate([value[rows * j : rows * (j + 1)] for j in range(value.shape[0] // rows)], axis=1)


def added(ref, rows=slice(None)):
    total = ref[0, rows].astype(F32)
    for i in range(1, ref.shape[0]):
        total = total + ref[i, rows].astype(F32)
    return total


def block(t):
    return slice(BLK * t, BLK * (t + 1))


def started(copies):
    for copy in copies:
        copy.start()
    return copies


def first_kernel(
    error_hbm, normed_hbm, cot_hbm, q_hbm, out_ref, local_ref, q_ref, cot_ref, normed_ref, error_ref, sems
):
    q_copy, cot_copy, normed_copy = started(
        [
            pltpu.make_async_copy(q_hbm, q_ref, sems.at[0]),
            pltpu.make_async_copy(cot_hbm, cot_ref, sems.at[1]),
            pltpu.make_async_copy(normed_hbm, normed_ref, sems.at[2]),
        ]
    )
    loads = started([pltpu.make_async_copy(error_hbm.at[k], error_ref.at[k], sems.at[3 + k]) for k in range(2)])
    q_copy.wait()
    q = [jnp.concatenate(pieces(q_ref[k], 3), axis=0) for k in range(2)]
    cot_copy.wait()
    for k in range(2):
        local_ref[4 + k] = cot_ref[k]
        token = dot(q[k], cot_ref[k], NT_DIMS)
        token = token[:RANK] + token[RANK : 2 * RANK] + token[2 * RANK :]
        token = jnp.concatenate([token, jnp.zeros((RANK, TOKP - TOK), F32)], axis=1)
        for t in range(NT):
            for j in range(3):
                first = ROWS * (4 + j) + RANK * k
                out_ref[t, first : first + RANK, :] = token[:, 128 * j : 128 * (j + 1)]
    normed_copy.wait()
    for j in range(4):
        local_ref[j] = normed_ref[:, 128 * j : 128 * (j + 1)]
    for k in range(2):
        loads[k].wait()
        for t in range(NT):
            part = dot(q[k], error_ref[k, block(t), :], NT_DIMS)
            part = part[:RANK] + part[RANK : 2 * RANK] + part[2 * RANK :]
            for j in range(4):
                first = ROWS * j + RANK * k
                out_ref[t, first : first + RANK, :] = part[:, 128 * j : 128 * (j + 1)]


def second_kernel(recv_ref, normed_ref, weight_ref, out_ref):
    total = added(recv_ref)
    token = jnp.concatenate(pieces(wide(total[4 * ROWS :], ROWS)[:, :TOK], 3), axis=0)
    grad = dot(token, normed_ref[...], NN_DIMS)
    factor = wide(total[: 4 * ROWS], ROWS) + (grad[:ROWS] + grad[ROWS : 2 * ROWS] + grad[2 * ROWS :])
    weight = [weight_ref[k].astype(F32) for k in range(2)]
    for m in range(NM):
        y = m // NL
        out_ref[m, :32, :] = tall(factor[8 * y : 8 * y + 8])
        for k in range(2):
            out_ref[m, 32 + 64 * k : 96 + 64 * k, :] = weight[k]


def third_kernel(recv_ref, out_ref, weight_ref):
    total = added(recv_ref, slice(0, 32))
    for z in range(NH):
        out_ref[z] = total
    for m in range(NM):
        weight_ref[m] = recv_ref[m, 32:, :].astype(BF16)


def repeat_kernel(scale, recv_ref, after_ref, out_ref):
    total = added(recv_ref)
    if scale != 1.0:
        total = total * scale
    total = total.astype(out_ref.dtype)
    for i in range(out_ref.shape[0]):
        out_ref[i] = total


def features(gathered_ref, t):
    return jnp.concatenate([gathered_ref[t, j] for j in range(4)], axis=1)


def basis_kernel(recv_ref, basis_ref, p_ref, v_ref):
    for y in range(NY):
        rows = slice(8 * (y % 2), 8 * (y % 2) + 8)
        for t in range(NT):
            value = wide(recv_ref[NT * y + t], 8)
            p_ref[y // 2, rows, block(t)] = value
            v_ref[y // 2, rows, block(t)] = value
    for i in range(RANK):
        vector = v_ref[:, i : i + 1, :]
        square = jnp.sum(vector * vector, axis=2, keepdims=True) + EPSILON
        if i < RANK - 1:
            rows = slice(8 * ((i + 1) // 8), RANK)
            coeff = jnp.sum(p_ref[:, rows, :] * vector, axis=2, keepdims=True)
        inverse = 1.0 / jnp.sqrt(square)
        column = vector * inverse
        basis_ref[:, i : i + 1, :] = column
        if i < RANK - 1:
            v_ref[:, rows, :] = v_ref[:, rows, :] - (coeff * inverse) * column


def term_kernel(basis_ref, gathered_ref, cot_ref, error_ref, term_ref):
    basis = [jnp.concatenate(pieces(basis_ref[k], 3), axis=0) for k in range(2)]
    both = jnp.concatenate(basis, axis=0)
    token = jnp.zeros((96, TOK), F32)
    for t in range(NT):
        token = token + dot(both[:, block(t)], features(gathered_ref, t), NT_DIMS)
    for k in range(2):
        part = token[48 * k : 48 * (k + 1)]
        part = part[:RANK] + part[RANK : 2 * RANK] + part[2 * RANK :]
        part = jnp.concatenate(pieces(part, 3), axis=0)
        term = dot(part, cot_ref[k], NN_DIMS) + dot(basis[k], error_ref[k], NN_DIMS)
        term = (term[:RANK] + term[RANK : 2 * RANK] + term[2 * RANK :]).astype(BF16)
        for z in range(NZ):
            term_ref[z, RANK * k : RANK * (k + 1), :] = term


def ready_kernel(gathered_hbm, flag_ref):
    flag_ref[...] = jnp.zeros((8, 128), F32)


def moment_kernel(core_ref, gathered_ref, cot_ref, error_ref, after_ref, moment_ref, mine_ref, flag_ref):
    flag_ref[...] = jnp.zeros((8, 128), F32)
    cot = jnp.concatenate([cot_ref[0], cot_ref[1]], axis=1)
    for t in range(NT):
        value = dot(features(gathered_ref, t), cot, TN_DIMS)
        for k in range(2):
            error = error_ref[k, block(t), :].astype(F32)
            moment_ref[k, block(t), :] = value[:, COL * k : COL * (k + 1)] + error
    core = core_ref[0]
    for x in range(NX):
        mine_ref[x] = jnp.concatenate([gathered_ref[NC * x + core, 4], gathered_ref[NC * x + core, 5]], axis=1)


def final_kernel(worker_ref, recv_ref, basis_ref, moment_ref, approx_ref, new_hbm, flag_ref, tile_ref, new_ref, sems):
    flag_ref[...] = jnp.zeros((8, 128), F32)
    parts = [pl.ds(D // 2 * i, D // 2) for i in range(2)]
    q_total = added(recv_ref) * (1.0 / WORKERS)
    zero = jnp.zeros((RANK, COL), BF16)
    right = []
    for k in range(2):
        q1, q2 = pieces(q_total[RANK * k : RANK * (k + 1)], 2)
        for q in (q1, q2, q1):
            right.append(jnp.concatenate([q, zero] if k == 0 else [zero, q], axis=1))
    right = jnp.concatenate(right, axis=0)

    def left_of(columns):
        left = []
        for k in range(2):
            b1, b2 = pieces(basis_ref[k, :, columns], 2)
            left += [b1, b1, b2]
        return jnp.concatenate(left, axis=0)

    worker = worker_ref[0]
    first = pl.multiple_of((worker // 2) * 128, 128)
    tile_ref[...] = dot(left_of(pl.ds(first, 128)), right, TN_DIMS)
    rows = tile_ref[pl.ds(pl.multiple_of((worker % 2) * 64, 64), 64), :]
    approx_ref[0] = rows[:, :COL].astype(BF16)
    approx_ref[1] = rows[:, COL:].astype(BF16)
    stores = []
    for t in range(NT):
        value = dot(left_of(block(t)), right, TN_DIMS)
        for k in range(2):
            part = moment_ref[k, block(t), :] - value[:, COL * k : COL * (k + 1)]
            new_ref[k, block(t), :] = part.astype(BF16)
        if t % 4 == 3:
            done = parts[t // 4]
            stores += started(
                [pltpu.make_async_copy(new_ref.at[:, done, :], new_hbm.at[:, done, :], sems.at[t // 4])]
            )
    for copy in stores:
        copy.wait()


def product_kernel(core_ref, cot_ref, weight_ref, after_ref, keep_ref, give_ref):
    core = core_ref[0]
    for half in range(2):
        first = 4 * (core if half else 1 - core)
        total = jnp.zeros((TOK, BLK), F32)
        for x in range(NX):
            weight = [
                weight_ref[pl.ds(first, 4), NL * x : NL * (x + 1), 64 * k : 64 * (k + 1), :].reshape(BLK, COL)
                for k in range(2)
            ]
            total = total + dot(cot_ref[x], jnp.concatenate(weight, axis=1), NT_DIMS)
        if half:
            keep_ref[...] = total
        else:
            give_ref[...] = total.astype(BF16)


def add_kernel(keep_ref, take_ref, out_ref):
    out_ref[...] = (keep_ref[...] + take_ref[...].astype(F32)).astype(BF16)


def exchange(value, axes):
    return lax.all_to_all(value, axes, 0, 0, tiled=True)


def shards(normed, kv_cotangent, kv_weight, error_buffer, q_factor):
    dma = pltpu.SemaphoreType.DMA
    error = error_buffer[0]
    core = lax.axis_index("core").astype(jnp.int32).reshape(1)
    worker = lax.axis_index(("y", "zh", "zl")).astype(jnp.int32).reshape(1)
    q_factor, core, worker = lax.optimization_barrier((q_factor, core, worker))

    swap = [(NX * i + j, NX * j + i) for i in range(NY) for j in range(NX)]
    weight = lax.ppermute(kv_weight, ("y", "x"), swap)
    flag = shape((8, 128))
    sent, local = call(
        first_kernel,
        (shape((NT, 7 * ROWS, 128)), shape((6, TOK, 128), BF16)),
        error,
        normed,
        kv_cotangent,
        q_factor,
        specs=[HBM] * 4,
        scratch=[
            pltpu.VMEM((2, RANK, COL), F32),
            pltpu.VMEM((2, TOK, COL), BF16),
            pltpu.VMEM((TOK, BLK), BF16),
            pltpu.VMEM((2, D, COL), BF16),
            dma((5,)),
        ],
        limit=BIG,
    )
    gathered = lax.all_gather(local, ("x", "core"), axis=0, tiled=False)
    ready = call(ready_kernel, flag, gathered, specs=[HBM], limit=BIG)
    other_core = [(0, 1), (1, 0)]
    recv = exchange(sent, ("x", "core"))
    recv = exchange(call(second_kernel, shape((NM, 160, 128)), recv, normed, weight), ("y", "zl"))
    sent, weight = call(third_kernel, (shape((NH, 32, 128)), shape((NM, 128, 128), BF16)), recv)
    weight = lax.all_gather(weight, "zh", axis=0, tiled=False)
    mean = functools.partial(repeat_kernel, 1.0 / WORKERS)
    sent = call(mean, shape((NY * NT, 32, 128)), exchange(sent, ("zh",)), ready)
    basis = call(
        basis_kernel,
        shape((2, RANK, D)),
        exchange(sent, ("y", "x", "core")),
        scratch=[pltpu.VMEM((2, RANK, D), F32), pltpu.VMEM((2, RANK, D), F32)],
        cost=(2**24, 12 * 2**20),
    )
    term = call(term_kernel, shape((NZ, ROWS, COL), BF16), basis, gathered, kv_cotangent, error)
    moment, mine, ready = call(
        moment_kernel,
        (shape((2, D, COL)), shape((NX, TOK, 2 * COL), BF16), flag),
        core,
        gathered,
        kv_cotangent,
        error,
        basis,
        specs=[SMEM] + [VMEM] * 4,
        cost=(2 * D * TOK * 2 * COL, 12 * 2**20),
    )
    repeat = functools.partial(repeat_kernel, 1.0)
    term = call(repeat, shape((NY, ROWS, COL)), exchange(term, ("zh", "zl")), ready, cost=(2**20, 12 * 2**20))
    approx, new_error, ready = call(
        final_kernel,
        (shape((2, 64, COL), BF16), shape((2, D, COL), BF16), flag),
        worker,
        exchange(term, ("y",)),
        basis,
        moment,
        specs=[SMEM] + [VMEM] * 3,
        outs=(VMEM, HBM, VMEM),
        scratch=[pltpu.VMEM((COL, 2 * COL), F32), pltpu.VMEM((2, D, COL), BF16), dma((2,))],
    )
    keep, give = call(
        product_kernel,
        (shape((TOK, BLK)), shape((TOK, BLK), BF16)),
        core,
        mine,
        weight,
        ready,
        specs=[SMEM, VMEM, VMEM, VMEM],
        cost=(2 * TOK * D * 2 * COL, 4 * 2**20),
    )
    take = lax.ppermute(give, "core", other_core)
    input_grad = call(add_kernel, shape((TOK, BLK), BF16), keep, take)
    return (input_grad, approx, new_error[None])


def solution(mesh):
    whole = Mesh(mesh.devices.reshape(NY, NH, NL, NX, NC), ("y", "zh", "zl", "x", "core"))
    dp, tensor = ("y", "zh", "zl"), ("x", "core")
    in_specs = (
        P(dp, tensor),
        P(None, dp, tensor),
        P(None, dp, tensor),
        P(dp, None, None, tensor),
        P(None, None, tensor),
    )
    out_specs = (P(dp, tensor), P(None, dp, tensor), P(dp, None, None, tensor))
    return jax.shard_map(shards, mesh=whole, in_specs=in_specs, out_specs=out_specs, check_vma=False)
```

```python
import jax
import jax.numpy as jnp
from jax import lax
from jax.experimental import pallas as pl
from jax.experimental.pallas import tpu as pltpu
from jax.sharding import Mesh
from jax.sharding import PartitionSpec as P

EPSILON = 1e-06
WORKERS = 64
NY, NH, NL, NX, NC = 4, 8, 2, 4, 2
NT = NX * NC
NM = NY * NL
BIG = 59 * 2**20
RANK = 16
ROWS = 2 * RANK
D = 4096
BLK = D // NT
TOK = 368
TOKP = 384
COL = 128
GCOL = BLK + 2 * COL
F32 = jnp.float32
BF16 = jnp.bfloat16
VMEM = pl.BlockSpec(memory_space=pltpu.VMEM)
SMEM = pl.BlockSpec(memory_space=pltpu.SMEM)
HBM = pl.BlockSpec(memory_space=pltpu.HBM)
NT_DIMS = (((1,), (1,)), ((), ()))
NN_DIMS = (((1,), (0,)), ((), ()))
TN_DIMS = (((0,), (0,)), ((), ()))


def dot(a, b, dims):
    return lax.dot_general(a, b, dims, preferred_element_type=F32)


def pieces(value, count):
    result = []
    for _ in range(count):
        part = value.astype(BF16)
        result.append(part)
        value = value - part.astype(F32)
    return result


def call(kernel, out_shape, *args, scratch=(), specs=None, outs=None, cost=None, limit=16 * 2**20):
    return pl.pallas_call(
        kernel,
        out_shape=out_shape,
        in_specs=specs or [VMEM] * len(args),
        out_specs=outs or jax.tree.map(lambda _: VMEM, out_shape),
        scratch_shapes=list(scratch),
        cost_estimate=cost and pl.CostEstimate(flops=cost[0], bytes_accessed=cost[1], transcendentals=0),
        compiler_params=pltpu.CompilerParams(vmem_limit_bytes=limit),
    )(*args)


def shape(dims, dtype=F32):
    return jax.ShapeDtypeStruct(dims, dtype)


def tall(value):
    return jnp.concatenate([value[:, 128 * j : 128 * (j + 1)] for j in range(value.shape[1] // 128)], axis=0)


def wide(value, rows):
    return jnp.concatenate([value[rows * j : rows * (j + 1)] for j in range(value.shape[0] // rows)], axis=1)


def added(ref, rows=slice(None)):
    total = ref[0, rows].astype(F32)
    for i in range(1, ref.shape[0]):
        total = total + ref[i, rows].astype(F32)
    return total


def block(t):
    return slice(BLK * t, BLK * (t + 1))


def started(copies):
    for copy in copies:
        copy.start()
    return copies


def first_kernel(
    error_hbm, normed_hbm, cot_hbm, q_hbm, out_ref, local_ref, q_ref, cot_ref, normed_ref, error_ref, sems
):
    q_copy, cot_copy, normed_copy = started(
        [
            pltpu.make_async_copy(q_hbm, q_ref, sems.at[0]),
            pltpu.make_async_copy(cot_hbm, cot_ref, sems.at[1]),
            pltpu.make_async_copy(normed_hbm, normed_ref, sems.at[2]),
        ]
    )
    loads = started([pltpu.make_async_copy(error_hbm.at[k], error_ref.at[k], sems.at[3 + k]) for k in range(2)])
    q_copy.wait()
    q = [jnp.concatenate(pieces(q_ref[k], 3), axis=0) for k in range(2)]
    cot_copy.wait()
    for k in range(2):
        local_ref[4 + k] = cot_ref[k]
        token = dot(q[k], cot_ref[k], NT_DIMS)
        token = token[:RANK] + token[RANK : 2 * RANK] + token[2 * RANK :]
        token = jnp.concatenate([token, jnp.zeros((RANK, TOKP - TOK), F32)], axis=1)
        for t in range(NT):
            for j in range(3):
                first = ROWS * (4 + j) + RANK * k
                out_ref[t, first : first + RANK, :] = token[:, 128 * j : 128 * (j + 1)]
    normed_copy.wait()
    for j in range(4):
        local_ref[j] = normed_ref[:, 128 * j : 128 * (j + 1)]
    for k in range(2):
        loads[k].wait()
        for t in range(NT):
            part = dot(q[k], error_ref[k, block(t), :], NT_DIMS)
            part = part[:RANK] + part[RANK : 2 * RANK] + part[2 * RANK :]
            for j in range(4):
                first = ROWS * j + RANK * k
                out_ref[t, first : first + RANK, :] = part[:, 128 * j : 128 * (j + 1)]


def second_kernel(recv_ref, normed_ref, weight_ref, out_ref):
    total = added(recv_ref)
    token = jnp.concatenate(pieces(wide(total[4 * ROWS :], ROWS)[:, :TOK], 3), axis=0)
    grad = dot(token, normed_ref[...], NN_DIMS)
    factor = wide(total[: 4 * ROWS], ROWS) + (grad[:ROWS] + grad[ROWS : 2 * ROWS] + grad[2 * ROWS :])
    for m in range(NM):
        y = m // NL
        high, low = pieces(tall(factor[8 * y : 8 * y + 8]), 2)
        out_ref[m, :32, :] = high
        out_ref[m, 32:64, :] = low
        for k in range(2):
            out_ref[m, 64 + 64 * k : 128 + 64 * k, :] = weight_ref[k]


def third_kernel(recv_ref, out_ref, weight_ref):
    total = added(recv_ref, slice(0, 32)) + added(recv_ref, slice(32, 64))
    for z in range(NH):
        out_ref[z] = total
    for m in range(NM):
        weight_ref[m] = recv_ref[m, 64:, :]


def repeat_kernel(recv_ref, out_ref):
    total = added(recv_ref).astype(out_ref.dtype)
    for i in range(out_ref.shape[0]):
        out_ref[i] = total


def mean_kernel(recv_ref, after_ref, out_ref):
    total = added(recv_ref) * (1.0 / WORKERS)
    for i in range(out_ref.shape[0]):
        out_ref[i] = total


def features(gathered_ref, t):
    return jnp.concatenate([gathered_ref[t, j] for j in range(4)], axis=1)


def basis_kernel(recv_ref, basis_ref, p_ref, v_ref):
    for y in range(NY):
        rows = slice(8 * (y % 2), 8 * (y % 2) + 8)
        for t in range(NT):
            value = wide(recv_ref[NT * y + t], 8)
            p_ref[y // 2, rows, block(t)] = value
            v_ref[y // 2, rows, block(t)] = value
    for i in range(RANK):
        vector = v_ref[:, i : i + 1, :]
        square = jnp.sum(vector * vector, axis=2, keepdims=True) + EPSILON
        if i < RANK - 1:
            rows = slice(8 * ((i + 1) // 8), RANK)
            coeff = jnp.sum(p_ref[:, rows, :] * vector, axis=2, keepdims=True)
        inverse = 1.0 / jnp.sqrt(square)
        column = vector * inverse
        basis_ref[:, i : i + 1, :] = column
        if i < RANK - 1:
            v_ref[:, rows, :] = v_ref[:, rows, :] - (coeff * inverse) * column


def term_kernel(basis_ref, high_ref, term_ref):
    for k in range(2):
        term = dot(jnp.concatenate(pieces(basis_ref[k], 3), axis=0), high_ref[k], NN_DIMS)
        term = (term[:RANK] + term[RANK : 2 * RANK] + term[2 * RANK :]).astype(BF16)
        for m in range(NM):
            term_ref[m, RANK * k : RANK * (k + 1), :] = term


def moment_kernel(core_ref, gathered_ref, cot_ref, error_ref, high_ref, low_ref, mine_ref, flag_ref):
    flag_ref[...] = jnp.zeros((8, 128), F32)
    cot = jnp.concatenate([cot_ref[0], cot_ref[1]], axis=1)
    for t in range(NT):
        value = dot(features(gathered_ref, t), cot, TN_DIMS)
        for k in range(2):
            moment = value[:, COL * k : COL * (k + 1)] + error_ref[k, block(t), :].astype(F32)
            high_ref[k, block(t), :], low_ref[k, block(t), :] = pieces(moment, 2)
    core = core_ref[0]
    for x in range(NX):
        mine_ref[x] = jnp.concatenate([gathered_ref[NC * x + core, 4], gathered_ref[NC * x + core, 5]], axis=1)


def final_kernel(
    worker_ref, recv_ref, basis_ref, high_ref, low_ref, approx_ref, new_hbm, flag_ref, tile_ref, new_ref, sems
):
    flag_ref[...] = jnp.zeros((8, 128), F32)
    parts = [pl.ds(D // 2 * i, D // 2) for i in range(2)]
    q_total = added(recv_ref) * (1.0 / WORKERS)
    zero = jnp.zeros((RANK, COL), BF16)
    right = []
    for k in range(2):
        q1, q2 = pieces(q_total[RANK * k : RANK * (k + 1)], 2)
        for q in (q1, q2, q1):
            right.append(jnp.concatenate([q, zero] if k == 0 else [zero, q], axis=1))
    right = jnp.concatenate(right, axis=0)

    def left_of(columns):
        left = []
        for k in range(2):
            b1, b2 = pieces(basis_ref[k, :, columns], 2)
            left += [b1, b1, b2]
        return jnp.concatenate(left, axis=0)

    worker = worker_ref[0]
    first = pl.multiple_of((worker // 2) * 128, 128)
    tile_ref[...] = dot(left_of(pl.ds(first, 128)), right, TN_DIMS)
    rows = tile_ref[pl.ds(pl.multiple_of((worker % 2) * 64, 64), 64), :]
    approx_ref[0] = rows[:, :COL].astype(BF16)
    approx_ref[1] = rows[:, COL:].astype(BF16)
    stores = []
    for t in range(NT):
        value = dot(left_of(block(t)), right, TN_DIMS)
        for k in range(2):
            part = high_ref[k, block(t), :].astype(F32) - value[:, COL * k : COL * (k + 1)]
            part = part + low_ref[k, block(t), :].astype(F32)
            new_ref[k, block(t), :] = part.astype(BF16)
        if t % 4 == 3:
            done = parts[t // 4]
            stores += started(
                [pltpu.make_async_copy(new_ref.at[:, done, :], new_hbm.at[:, done, :], sems.at[t // 4])]
            )
    for copy in stores:
        copy.wait()


def product_kernel(core_ref, cot_ref, weight_ref, after_ref, keep_ref, give_ref):
    core = core_ref[0]
    for half in range(2):
        first = 4 * (core if half else 1 - core)
        total = jnp.zeros((TOK, BLK), F32)
        for x in range(NX):
            weight = [
                weight_ref[pl.ds(first, 4), NL * x : NL * (x + 1), 64 * k : 64 * (k + 1), :].reshape(BLK, COL)
                for k in range(2)
            ]
            total = total + dot(cot_ref[x], jnp.concatenate(weight, axis=1), NT_DIMS)
        if half:
            keep_ref[...] = total
        else:
            give_ref[...] = total.astype(BF16)


def add_kernel(keep_ref, take_ref, out_ref):
    out_ref[...] = (keep_ref[...] + take_ref[...].astype(F32)).astype(BF16)


def exchange(value, axes):
    return lax.all_to_all(value, axes, 0, 0, tiled=True)


def shards(normed, kv_cotangent, kv_weight, error_buffer, q_factor):
    dma = pltpu.SemaphoreType.DMA
    error = error_buffer[0]
    core = lax.axis_index("core").astype(jnp.int32).reshape(1)
    worker = lax.axis_index(("y", "zh", "zl")).astype(jnp.int32).reshape(1)
    q_factor, core, worker = lax.optimization_barrier((q_factor, core, worker))

    swap = [(NX * i + j, NX * j + i) for i in range(NY) for j in range(NX)]
    weight = lax.ppermute(kv_weight, ("y", "x"), swap)
    sent, local = call(
        first_kernel,
        (shape((NT, 7 * ROWS, 128)), shape((6, TOK, 128), BF16)),
        error,
        normed,
        kv_cotangent,
        q_factor,
        specs=[HBM] * 4,
        scratch=[
            pltpu.VMEM((2, RANK, COL), F32),
            pltpu.VMEM((2, TOK, COL), BF16),
            pltpu.VMEM((TOK, BLK), BF16),
            pltpu.VMEM((2, D, COL), BF16),
            dma((5,)),
        ],
        limit=BIG,
    )
    gathered = lax.all_gather(local, ("x", "core"), axis=0, tiled=False)
    recv = exchange(sent, ("x", "core"))
    recv = exchange(call(second_kernel, shape((NM, 192, 128), BF16), recv, normed, weight), ("y", "zl"))
    sent, weight = call(third_kernel, (shape((NH, 32, 128)), shape((NM, 128, 128), BF16)), recv)
    weight = lax.all_gather(weight, "zh", axis=0, tiled=False)
    high, low, mine, ready = call(
        moment_kernel,
        (shape((2, D, COL), BF16), shape((2, D, COL), BF16), shape((NX, TOK, 2 * COL), BF16), shape((8, 128))),
        core,
        gathered,
        kv_cotangent,
        error,
        specs=[SMEM] + [VMEM] * 3,
        cost=(2 * D * TOK * 2 * COL, 12 * 2**20),
    )
    sent = call(mean_kernel, shape((NY * NT, 32, 128)), exchange(sent, ("zh",)), ready)
    basis = call(
        basis_kernel,
        shape((2, RANK, D)),
        exchange(sent, ("y", "x", "core")),
        scratch=[pltpu.VMEM((2, RANK, D), F32), pltpu.VMEM((2, RANK, D), F32)],
        cost=(2**24, 12 * 2**20),
    )
    term = call(term_kernel, shape((NM, ROWS, COL), BF16), basis, high)
    term = call(repeat_kernel, shape((NH, ROWS, COL), BF16), exchange(term, ("y", "zl")))
    approx, new_error, ready = call(
        final_kernel,
        (shape((2, 64, COL), BF16), shape((2, D, COL), BF16), shape((8, 128))),
        worker,
        exchange(term, ("zh",)),
        basis,
        high,
        low,
        specs=[SMEM] + [VMEM] * 4,
        outs=(VMEM, HBM, VMEM),
        scratch=[pltpu.VMEM((COL, 2 * COL), F32), pltpu.VMEM((2, D, COL), BF16), dma((2,))],
    )
    keep, give = call(
        product_kernel,
        (shape((TOK, BLK)), shape((TOK, BLK), BF16)),
        core,
        mine,
        weight,
        ready,
        specs=[SMEM] + [VMEM] * 3,
        cost=(2 * TOK * D * 2 * COL, 4 * 2**20),
    )
    take = lax.ppermute(give, "core", [(0, 1), (1, 0)])
    input_grad = call(add_kernel, shape((TOK, BLK), BF16), keep, take)
    return (input_grad, approx, new_error[None])


def solution(mesh):
    whole = Mesh(mesh.devices.reshape(NY, NH, NL, NX, NC), ("y", "zh", "zl", "x", "core"))
    dp, tensor = ("y", "zh", "zl"), ("x", "core")
    in_specs = (
        P(dp, tensor),
        P(None, dp, tensor),
        P(None, dp, tensor),
        P(dp, None, None, tensor),
        P(None, None, tensor),
    )
    out_specs = (P(dp, tensor), P(None, dp, tensor), P(dp, None, None, tensor))
    return jax.shard_map(shards, mesh=whole, in_specs=in_specs, out_specs=out_specs, check_vma=False)
```

```python
import jax
import jax.numpy as jnp
from jax import lax
from jax.experimental import pallas as pl
from jax.experimental.pallas import tpu as pltpu
from jax.sharding import Mesh
from jax.sharding import PartitionSpec as P

EPSILON = 1e-06
WORKERS = 64
NY, NH, NL, NX, NC = 4, 8, 2, 4, 2
NT = NX * NC
NM = NY * NL
BIG = 59 * 2**20
RANK = 16
ROWS = 2 * RANK
D = 4096
BLK = D // NT
TOK = 368
TOKP = 384
COL = 128
GCOL = BLK + 2 * COL
F32 = jnp.float32
BF16 = jnp.bfloat16
VMEM = pl.BlockSpec(memory_space=pltpu.VMEM)
SMEM = pl.BlockSpec(memory_space=pltpu.SMEM)
HBM = pl.BlockSpec(memory_space=pltpu.HBM)
NT_DIMS = (((1,), (1,)), ((), ()))
NN_DIMS = (((1,), (0,)), ((), ()))
TN_DIMS = (((0,), (0,)), ((), ()))


def dot(a, b, dims):
    return lax.dot_general(a, b, dims, preferred_element_type=F32)


def pieces(value, count):
    result = []
    for _ in range(count):
        part = value.astype(BF16)
        result.append(part)
        value = value - part.astype(F32)
    return result


def call(kernel, out_shape, *args, scratch=(), specs=None, outs=None, cost=None, limit=16 * 2**20):
    return pl.pallas_call(
        kernel,
        out_shape=out_shape,
        in_specs=specs or [VMEM] * len(args),
        out_specs=outs or jax.tree.map(lambda _: VMEM, out_shape),
        scratch_shapes=list(scratch),
        cost_estimate=cost and pl.CostEstimate(flops=cost[0], bytes_accessed=cost[1], transcendentals=0),
        compiler_params=pltpu.CompilerParams(vmem_limit_bytes=limit),
    )(*args)


def shape(dims, dtype=F32):
    return jax.ShapeDtypeStruct(dims, dtype)


def tall(value):
    return jnp.concatenate([value[:, 128 * j : 128 * (j + 1)] for j in range(value.shape[1] // 128)], axis=0)


def wide(value, rows):
    return jnp.concatenate([value[rows * j : rows * (j + 1)] for j in range(value.shape[0] // rows)], axis=1)


def added(ref, rows=slice(None)):
    total = ref[0, rows].astype(F32)
    for i in range(1, ref.shape[0]):
        total = total + ref[i, rows].astype(F32)
    return total


def block(t):
    return slice(BLK * t, BLK * (t + 1))


def started(copies):
    for copy in copies:
        copy.start()
    return copies


def first_kernel(
    error_hbm, normed_hbm, cot_hbm, q_hbm, out_ref, local_ref, q_ref, cot_ref, normed_ref, error_ref, sems
):
    q_copy, cot_copy, normed_copy = started(
        [
            pltpu.make_async_copy(q_hbm, q_ref, sems.at[0]),
            pltpu.make_async_copy(cot_hbm, cot_ref, sems.at[1]),
            pltpu.make_async_copy(normed_hbm, normed_ref, sems.at[2]),
        ]
    )
    loads = started([pltpu.make_async_copy(error_hbm.at[k], error_ref.at[k], sems.at[3 + k]) for k in range(2)])
    q_copy.wait()
    q = [jnp.concatenate(pieces(q_ref[k], 3), axis=0) for k in range(2)]
    cot_copy.wait()
    for k in range(2):
        local_ref[4 + k] = cot_ref[k]
        token = dot(q[k], cot_ref[k], NT_DIMS)
        token = token[:RANK] + token[RANK : 2 * RANK] + token[2 * RANK :]
        token = jnp.concatenate([token, jnp.zeros((RANK, TOKP - TOK), F32)], axis=1)
        for t in range(NT):
            for j in range(3):
                first = ROWS * (4 + j) + RANK * k
                out_ref[t, first : first + RANK, :] = token[:, 128 * j : 128 * (j + 1)]
    normed_copy.wait()
    for j in range(4):
        local_ref[j] = normed_ref[:, 128 * j : 128 * (j + 1)]
    for k in range(2):
        loads[k].wait()
        for t in range(NT):
            part = dot(q[k], error_ref[k, block(t), :], NT_DIMS)
            part = part[:RANK] + part[RANK : 2 * RANK] + part[2 * RANK :]
            for j in range(4):
                first = ROWS * j + RANK * k
                out_ref[t, first : first + RANK, :] = part[:, 128 * j : 128 * (j + 1)]


def second_kernel(recv_ref, normed_ref, weight_ref, out_ref):
    total = added(recv_ref)
    token = jnp.concatenate(pieces(wide(total[4 * ROWS :], ROWS)[:, :TOK], 3), axis=0)
    grad = dot(token, normed_ref[...], NN_DIMS)
    factor = wide(total[: 4 * ROWS], ROWS) + (grad[:ROWS] + grad[ROWS : 2 * ROWS] + grad[2 * ROWS :])
    for m in range(NM):
        y = m // NL
        high, low = pieces(tall(factor[8 * y : 8 * y + 8]), 2)
        out_ref[m, :32, :] = high
        out_ref[m, 32:64, :] = low
        for k in range(2):
            out_ref[m, 64 + 64 * k : 128 + 64 * k, :] = weight_ref[k]


def third_kernel(recv_ref, out_ref, weight_ref):
    total = added(recv_ref, slice(0, 32)) + added(recv_ref, slice(32, 64))
    high, low = pieces(total, 2)
    for z in range(NH):
        out_ref[z, :32, :] = high
        out_ref[z, 32:, :] = low
    for m in range(NM):
        weight_ref[m] = recv_ref[m, 64:, :]


def repeat_kernel(recv_ref, out_ref):
    total = added(recv_ref).astype(out_ref.dtype)
    for i in range(out_ref.shape[0]):
        out_ref[i] = total


def mean_kernel(recv_ref, after_ref, out_ref):
    total = (added(recv_ref, slice(0, 32)) + added(recv_ref, slice(32, 64))) * (1.0 / WORKERS)
    high, low = pieces(total, 2)
    for i in range(out_ref.shape[0]):
        out_ref[i, :32, :] = high
        out_ref[i, 32:, :] = low


def features(gathered_ref, t):
    return jnp.concatenate([gathered_ref[t, j] for j in range(4)], axis=1)


def basis_kernel(recv_ref, basis_ref, p_ref, v_ref):
    for y in range(NY):
        rows = slice(8 * (y % 2), 8 * (y % 2) + 8)
        for t in range(NT):
            place = NT * y + t
            value = wide(recv_ref[place, :32].astype(F32) + recv_ref[place, 32:].astype(F32), 8)
            p_ref[y // 2, rows, block(t)] = value
            v_ref[y // 2, rows, block(t)] = value
    for i in range(RANK):
        vector = v_ref[:, i : i + 1, :]
        square = jnp.sum(vector * vector, axis=2, keepdims=True) + EPSILON
        if i < RANK - 1:
            rows = slice(8 * ((i + 1) // 8), RANK)
            coeff = jnp.sum(p_ref[:, rows, :] * vector, axis=2, keepdims=True)
        inverse = 1.0 / jnp.sqrt(square)
        column = vector * inverse
        basis_ref[:, i : i + 1, :] = column
        if i < RANK - 1:
            v_ref[:, rows, :] = v_ref[:, rows, :] - (coeff * inverse) * column


def term_kernel(basis_ref, high_ref, term_ref):
    for k in range(2):
        term = dot(jnp.concatenate(pieces(basis_ref[k], 3), axis=0), high_ref[k], NN_DIMS)
        term = (term[:RANK] + term[RANK : 2 * RANK] + term[2 * RANK :]).astype(BF16)
        for m in range(NM):
            term_ref[m, RANK * k : RANK * (k + 1), :] = term


def moment_kernel(core_ref, gathered_ref, cot_ref, error_ref, high_ref, low_ref, mine_ref, flag_ref):
    flag_ref[...] = jnp.zeros((8, 128), F32)
    cot = jnp.concatenate([cot_ref[0], cot_ref[1]], axis=1)
    for t in range(NT):
        value = dot(features(gathered_ref, t), cot, TN_DIMS)
        for k in range(2):
            moment = value[:, COL * k : COL * (k + 1)] + error_ref[k, block(t), :].astype(F32)
            high_ref[k, block(t), :], low_ref[k, block(t), :] = pieces(moment, 2)
    core = core_ref[0]
    for x in range(NX):
        mine_ref[x] = jnp.concatenate([gathered_ref[NC * x + core, 4], gathered_ref[NC * x + core, 5]], axis=1)


def final_kernel(
    worker_ref, recv_ref, basis_ref, high_ref, low_ref, approx_ref, new_hbm, flag_ref, tile_ref, new_ref, sems
):
    flag_ref[...] = jnp.zeros((8, 128), F32)
    parts = [pl.ds(D // 2 * i, D // 2) for i in range(2)]
    q_total = added(recv_ref) * (1.0 / WORKERS)
    zero = jnp.zeros((RANK, COL), BF16)
    right = []
    for k in range(2):
        q1, q2 = pieces(q_total[RANK * k : RANK * (k + 1)], 2)
        for q in (q1, q2, q1):
            right.append(jnp.concatenate([q, zero] if k == 0 else [zero, q], axis=1))
    right = jnp.concatenate(right, axis=0)

    def left_of(columns):
        left = []
        for k in range(2):
            b1, b2 = pieces(basis_ref[k, :, columns], 2)
            left += [b1, b1, b2]
        return jnp.concatenate(left, axis=0)

    worker = worker_ref[0]
    first = pl.multiple_of((worker // 2) * 128, 128)
    tile_ref[...] = dot(left_of(pl.ds(first, 128)), right, TN_DIMS)
    rows = tile_ref[pl.ds(pl.multiple_of((worker % 2) * 64, 64), 64), :]
    approx_ref[0] = rows[:, :COL].astype(BF16)
    approx_ref[1] = rows[:, COL:].astype(BF16)
    stores = []
    for t in range(NT):
        value = dot(left_of(block(t)), right, TN_DIMS)
        for k in range(2):
            part = high_ref[k, block(t), :].astype(F32) - value[:, COL * k : COL * (k + 1)]
            part = part + low_ref[k, block(t), :].astype(F32)
            new_ref[k, block(t), :] = part.astype(BF16)
        if t % 4 == 3:
            done = parts[t // 4]
            stores += started(
                [pltpu.make_async_copy(new_ref.at[:, done, :], new_hbm.at[:, done, :], sems.at[t // 4])]
            )
    for copy in stores:
        copy.wait()


def product_kernel(core_ref, cot_ref, weight_ref, after_ref, keep_ref, give_ref):
    core = core_ref[0]
    for half in range(2):
        first = 4 * (core if half else 1 - core)
        total = jnp.zeros((TOK, BLK), F32)
        for x in range(NX):
            weight = [
                weight_ref[pl.ds(first, 4), NL * x : NL * (x + 1), 64 * k : 64 * (k + 1), :].reshape(BLK, COL)
                for k in range(2)
            ]
            total = total + dot(cot_ref[x], jnp.concatenate(weight, axis=1), NT_DIMS)
        if half:
            keep_ref[...] = total
        else:
            give_ref[...] = total.astype(BF16)


def add_kernel(keep_ref, take_ref, out_ref):
    out_ref[...] = (keep_ref[...] + take_ref[...].astype(F32)).astype(BF16)


def exchange(value, axes):
    return lax.all_to_all(value, axes, 0, 0, tiled=True)


def shards(normed, kv_cotangent, kv_weight, error_buffer, q_factor):
    dma = pltpu.SemaphoreType.DMA
    error = error_buffer[0]
    core = lax.axis_index("core").astype(jnp.int32).reshape(1)
    worker = lax.axis_index(("y", "zh", "zl")).astype(jnp.int32).reshape(1)
    q_factor, core, worker = lax.optimization_barrier((q_factor, core, worker))

    swap = [(NX * i + j, NX * j + i) for i in range(NY) for j in range(NX)]
    weight = lax.ppermute(kv_weight, ("y", "x"), swap)
    sent, local = call(
        first_kernel,
        (shape((NT, 7 * ROWS, 128)), shape((6, TOK, 128), BF16)),
        error,
        normed,
        kv_cotangent,
        q_factor,
        specs=[HBM] * 4,
        scratch=[
            pltpu.VMEM((2, RANK, COL), F32),
            pltpu.VMEM((2, TOK, COL), BF16),
            pltpu.VMEM((TOK, BLK), BF16),
            pltpu.VMEM((2, D, COL), BF16),
            dma((5,)),
        ],
        limit=BIG,
    )
    gathered = lax.all_gather(local, ("x", "core"), axis=0, tiled=False)
    recv = exchange(sent, ("x", "core"))
    recv = exchange(call(second_kernel, shape((NM, 192, 128), BF16), recv, normed, weight), ("y", "zl"))
    sent, weight = call(third_kernel, (shape((NH, 64, 128), BF16), shape((NM, 128, 128), BF16)), recv)
    weight = lax.all_gather(weight, "zh", axis=0, tiled=False)
    high, low, mine, ready = call(
        moment_kernel,
        (shape((2, D, COL), BF16), shape((2, D, COL), BF16), shape((NX, TOK, 2 * COL), BF16), shape((8, 128))),
        core,
        gathered,
        kv_cotangent,
        error,
        specs=[SMEM] + [VMEM] * 3,
        cost=(2 * D * TOK * 2 * COL, 12 * 2**20),
    )
    sent = call(mean_kernel, shape((NY * NT, 64, 128), BF16), exchange(sent, ("zh",)), ready)
    basis = call(
        basis_kernel,
        shape((2, RANK, D)),
        exchange(sent, ("y", "x", "core")),
        scratch=[pltpu.VMEM((2, RANK, D), F32), pltpu.VMEM((2, RANK, D), F32)],
        cost=(2**24, 12 * 2**20),
    )
    term = call(term_kernel, shape((NM, ROWS, COL), BF16), basis, high)
    term = call(repeat_kernel, shape((NH, ROWS, COL), BF16), exchange(term, ("y", "zl")))
    approx, new_error, ready = call(
        final_kernel,
        (shape((2, 64, COL), BF16), shape((2, D, COL), BF16), shape((8, 128))),
        worker,
        exchange(term, ("zh",)),
        basis,
        high,
        low,
        specs=[SMEM] + [VMEM] * 4,
        outs=(VMEM, HBM, VMEM),
        scratch=[pltpu.VMEM((COL, 2 * COL), F32), pltpu.VMEM((2, D, COL), BF16), dma((2,))],
    )
    keep, give = call(
        product_kernel,
        (shape((TOK, BLK)), shape((TOK, BLK), BF16)),
        core,
        mine,
        weight,
        ready,
        specs=[SMEM] + [VMEM] * 3,
        cost=(2 * TOK * D * 2 * COL, 4 * 2**20),
    )
    take = lax.ppermute(give, "core", [(0, 1), (1, 0)])
    input_grad = call(add_kernel, shape((TOK, BLK), BF16), keep, take)
    return (input_grad, approx, new_error[None])


def solution(mesh):
    whole = Mesh(mesh.devices.reshape(NY, NH, NL, NX, NC), ("y", "zh", "zl", "x", "core"))
    dp, tensor = ("y", "zh", "zl"), ("x", "core")
    in_specs = (
        P(dp, tensor),
        P(None, dp, tensor),
        P(None, dp, tensor),
        P(dp, None, None, tensor),
        P(None, None, tensor),
    )
    out_specs = (P(dp, tensor), P(None, dp, tensor), P(dp, None, None, tensor))
    return jax.shard_map(shards, mesh=whole, in_specs=in_specs, out_specs=out_specs, check_vma=False)
```
